128 devices in a mesh: gx: 16 (over y, x), gy: 8 (over z, core).
Axes of the slice: x: 4, y: 4, z: 4, core: 2. Of those that a mesh axis runs over, the one named last changes fastest.
Arguments:
- volume: bfloat16 [96, 64, 128, 128], P('gx', None, 'gy'), may hold values from -6 to 6
- weight3: bfloat16 [128, 27, 64], replicated, may hold values from -0.15625 to 0.15625
- bias3: bfloat16 [128], replicated, may hold values from -4 to 4
- weight4: bfloat16 [256, 27, 128], P('gy', None, 'gx'), may hold values from -0.109375 to 0.109375
- bias4: bfloat16 [256], P('gy'), may hold values from -3 to 3
Outputs:
- encoded: bfloat16 [48, 256, 4096], P('gx', 'gy')
The draws below stay inside these ranges and needn't reach their ends.
All inputs are finite; a program needn't handle non-finite values.
Results may differ from the reference program's by a relative error of at most 0.015.
Values may be sent and summed in bfloat16 or wider, within the bound.
A program may use at most 384 MiB of HBM per device.

```python
import jax
import jax.numpy as jnp
from jax import lax

C3IN = 64
C3OUT = 128
C4OUT = 256
SIDE = 128
DEPTH = 96


def shard_levels(key, dims, cuts, least, largest):
    gain = 1.0
    for axis_at, blocks in cuts:
        steps = jax.random.uniform(jax.random.fold_in(jax.random.fold_in(key, 6), axis_at), (blocks,), jnp.float32, least / len(cuts), largest / len(cuts))
        gain = gain * jnp.repeat(jnp.exp(steps), dims[axis_at] // blocks).reshape((-1,) + (1,) * (len(dims) - 1 - axis_at))
    return gain


def normal_values(rng, extent, scale, limit, cuts=(), held_as=jnp.bfloat16):
    factor_of = shard_levels(rng, extent, cuts, -0.22, 0.18) if cuts else 1.0
    array = jax.random.normal(rng, extent, jnp.float32) * scale * factor_of
    return jnp.minimum(jnp.maximum(array, -limit), limit).astype(held_as)


def setup_inputs(seed: int = 0) -> dict:
    streams_of = jax.random.split(jax.random.key(seed), 6)
    return {
        "volume": normal_values(streams_of[0], (DEPTH, C3IN, SIDE, SIDE), 1.0, 6.0, ((0, 16), (2, 8))),
        "weight3": normal_values(streams_of[1], (C3OUT, 27, C3IN), (27 * C3IN) ** -0.5, 0.15625),
        "bias3": normal_values(streams_of[2], (C3OUT,), 1.0, 4.0),
        "weight4": normal_values(streams_of[3], (C4OUT, 27, C3OUT), (27 * C3OUT) ** -0.5, 0.109375, ((0, 8), (2, 16))),
        "bias4": normal_values(streams_of[4], (C4OUT,), 0.5, 3.0, ((0, 8),)),
    }


def convolve(field, weight, bias):
    outs = weight.shape[0]
    ins = weight.shape[2]
    kernel = weight.astype(jnp.float32).reshape(outs, 3, 3, 3, ins).transpose(0, 4, 1, 2, 3)
    result = lax.conv_general_dilated(field[None], kernel, (1, 1, 1), ((1, 1), (1, 1), (1, 1)), dimension_numbers=("NCDHW", "OIDHW", "NCDHW"), precision=lax.Precision.HIGHEST)[0]
    return result + bias.astype(jnp.float32)[:, None, None, None]


def reference(volume, weight3, bias3, weight4, bias4):
    field = volume.astype(jnp.float32).transpose(1, 0, 2, 3)
    conv3 = convolve(field, weight3, bias3)
    chans, depth, height, width = conv3.shape
    active = jnp.maximum(conv3, 0.0).reshape(chans, depth // 2, 2, height // 2, 2, width // 2, 2)
    pooled = jnp.max(active, axis=(2, 4, 6)).astype(jnp.bfloat16)
    conv4 = convolve(pooled.astype(jnp.float32), weight4, bias4)
    leaky = jnp.where(conv4 > 0, conv4, 0.3 * conv4)
    outs, planes, rows, cols = leaky.shape
    return leaky.transpose(1, 0, 2, 3).reshape(planes, outs, rows * cols).astype(jnp.bfloat16)
```

```python
import jax
import jax.numpy as jnp
from jax import lax
from jax.experimental import pallas as pl
from jax.experimental.pallas import tpu as pltpu
from jax.sharding import PartitionSpec as P

MESH = pl.DeviceIdType.MESH
F32 = jnp.float32
BF16 = jnp.bfloat16
NT = (((1,), (1,)), ((), ()))
NX = 16
NY = 8


def remote(src, dst, send, recv, gx, gy):
    return pltpu.make_async_remote_copy(
        src_ref=src, dst_ref=dst, send_sem=send, recv_sem=recv, device_id=(gx, gy), device_id_type=MESH
    )


def loop(count, step):
    lax.fori_loop(0, count, lambda i, c: (step(i), c)[1], 0)


def kernel(
    vol, w3, b3, w4, b4, out,
    v, rh, vs, tt, xt, rr, w3f, w3n, x4, ph, pr, pt, ws, ga, ff, wk, ob,
    lsem, hs, hr, rs, rrs, as_, ar, bs, br, fs, fr, phs, phr, prs, prr, os_, or_, ol,
):
    gx = lax.axis_index("gx")
    gy = lax.axis_index("gy")
    xup, xdn = lax.rem(gx + 1, NX), lax.rem(gx + NX - 1, NX)
    yup, ydn = lax.rem(gy + 1, NY), lax.rem(gy + NY - 1, NY)
    sib = gy + 1 - 2 * lax.rem(gy, 2)
    has_xdn = (gx > 0).astype(F32)
    has_xup = (gx < NX - 1).astype(F32)
    has_ydn = (gy > 0).astype(F32)
    has_yup = (gy < NY - 1).astype(F32)

    barrier = pltpu.get_barrier_semaphore()

    def greet_x(k):
        pl.semaphore_signal(barrier, inc=1, device_id=(lax.rem(gx + k + 1, NX), gy), device_id_type=MESH)

    def greet_y(k):
        pl.semaphore_signal(barrier, inc=1, device_id=(gx, lax.rem(gy + k + 1, NY)), device_id_type=MESH)

    loop(NX - 1, greet_x)
    loop(NY - 1, greet_y)
    local_vol = pltpu.make_async_copy(vol, v, lsem)
    local_vol.start()

    ws[...] = jnp.zeros_like(ws)
    for o in range(32):
        ws[o * 32 : o * 32 + 27, 0:8] = w4[o].astype(F32)
    eye = lax.broadcasted_iota(jnp.int32, (32, 32), 0) == lax.broadcasted_iota(jnp.int32, (32, 32), 1)
    bcol = jnp.sum(jnp.where(eye, b4[...].astype(F32), 0.0), axis=1, keepdims=True)
    lane0 = lax.broadcasted_iota(jnp.int32, (32, 128), 1) == 0
    ws[pl.ds(27, 32, 32), :] = jnp.where(lane0, bcol, 0.0)
    row = lax.broadcasted_iota(jnp.int32, (128, 128), 0)
    col = lax.broadcasted_iota(jnp.int32, (128, 128), 1)
    spread = jnp.where((col % 8 == row), 1.0, 0.0).astype(BF16)
    rep = lax.dot_general(ws[...].astype(BF16), spread, (((1,), (0,)), ((), ())), preferred_element_type=F32)
    rep = rep.reshape(2, 16, 32, 128)
    group = lax.broadcasted_iota(jnp.int32, (2, 32, 128), 2) // 8
    packed = jnp.zeros((2, 32, 128), F32)
    for b in range(16):
        packed = packed + jnp.where(group == b, rep[:, b], 0.0)
    ga[gx] = packed.reshape(64, 128).astype(BF16)

    pl.semaphore_wait(barrier, NX - 1 + NY - 1)

    plane_up = remote(vol.at[5], rh.at[0], hs.at[0], hr.at[0], xup, gy)
    plane_dn = remote(vol.at[0], rh.at[1], hs.at[1], hr.at[1], xdn, gy)
    plane_up.start()
    plane_dn.start()

    def gather_x(k):
        return remote(ga.at[gx], ga.at[gx], as_.at[k], ar.at[k], lax.rem(gx + k + 1, NX), gy)

    def gather_x_in(k):
        src = lax.rem(gx + NX - k - 1, NX)
        return remote(ga.at[src], ga.at[src], as_.at[k], ar.at[k], gx, gy)

    loop(NX - 1, lambda k: gather_x(k).start())

    w3f[...] = jnp.zeros_like(w3f)

    def widen(o):
        w3f[pl.ds(o * 32, 27), 0:64] = w3[o].astype(F32)

    loop(128, widen)
    for n in range(9):
        k0, k1, k2 = (w3f[pl.ds(9 * kd + n, 128, 32), :][:, 0:64] for kd in range(3))
        z = jnp.zeros((128, 64), F32)
        w3n[0:128, n * 256 : n * 256 + 256] = jnp.concatenate([k0, k1, k2, z], 1).astype(BF16)
        w3n[128:256, n * 256 : n * 256 + 256] = jnp.concatenate([z, k0, k1, k2], 1).astype(BF16)

    tt[...] = jnp.zeros_like(tt)

    def load_plane(src, half, scale):
        def step(i):
            x = src[pl.ds(i * 8, 8)].astype(F32)
            if scale is not None:
                x = x * scale
            vs[pl.ds(half * 1024 + i * 128, 128), :] = x.reshape(128, 128)

        loop(8, step)

    def turn(j):
        def step(i):
            for u in range(4):
                h = i * 4 + u
                tt[u, 8:136] = vs[pl.ds(h, 128, 16), :].T
                for kw in range(3):
                    xt[kw, j, h + 1] = tt[u, 7 + kw : 135 + kw].astype(BF16)

        loop(4, step)

    def rows_out(n, js, count):
        up = remote(xt.at[1, pl.ds(js, count), 16], rr.at[0, pl.ds(js, count)], rs.at[n, 0], rrs.at[n, 0], gx, yup)
        dn = remote(xt.at[1, pl.ds(js, count), 1], rr.at[1, pl.ds(js, count)], rs.at[n, 1], rrs.at[n, 1], gx, ydn)
        return up, dn

    def place_row(d, j):
        tt[0, 8:136] = rr[d, j].astype(F32) * (has_ydn if d == 0 else has_yup)
        for kw in range(3):
            xt[kw, j, 17 * d] = tt[0, 7 + kw : 135 + kw].astype(BF16)

    local_vol.wait()
    for j in (1, 2):
        load_plane(v.at[2 * j - 1], 0, None)
        load_plane(v.at[2 * j], 1, None)
        turn(j)
    inner = rows_out(0, 1, 2)
    for c in inner:
        c.start()

    def section3(j, half):
        top = 8 * half
        acc = None
        for kh in range(3):
            parts = []
            for kw in range(3):
                parts.append(xt[kw, j, pl.ds(top + kh, 8)].reshape(1024, 128))
                parts.append(xt[kw, j + 1, pl.ds(top + kh, 8)].reshape(1024, 128))
            d = lax.dot_general(
                jnp.concatenate(parts, 1), w3n[:, kh * 768 : (kh + 1) * 768], NT, preferred_element_type=F32
            )
            acc = d if acc is None else acc + d
        m = jnp.maximum(acc[:, :128], acc[:, 128:]).reshape(4, 2, 128, 128)
        bias = b3[...].astype(F32)
        for q in range(4):
            pt[q] = jnp.maximum(m[q, 0], m[q, 1])
            p = jnp.maximum(pt[q, pl.ds(0, 64, 2), :], pt[q, pl.ds(1, 64, 2), :])
            place_pooled(jnp.maximum(p + bias, 0.0), j + 1, half * 4 + q + 1)

    def place_pooled(p, plane, r):
        z = jnp.zeros((1, 128), F32)
        x4[0, plane, r] = jnp.concatenate([z, p[:-1]], 0).astype(BF16)
        x4[1, plane, r] = p.astype(BF16)
        x4[2, plane, r] = jnp.concatenate([p[1:], z], 0).astype(BF16)

    for c in inner:
        c.wait_recv()
    for j in (1, 2):
        for d in range(2):
            place_row(d, j)
    section3(1, 0)

    loop(NX - 1, lambda k: gather_x_in(k).wait_recv())
    lane_group = lax.broadcasted_iota(jnp.int32, (16, 128), 1) // 8

    def swap(q):
        a = [ga[i, pl.ds(pl.multiple_of(q * 16, 16), 16)].astype(F32) for i in range(16)]
        for s in (1, 2, 4, 8):
            low = (lane_group // s) % 2 == 0
            nxt = list(a)
            for i in range(16):
                if i & s == 0:
                    nxt[i] = jnp.where(low, a[i], pltpu.roll(a[i + s], 8 * s, 1))
                    nxt[i + s] = jnp.where(low, pltpu.roll(a[i], 128 - 8 * s, 1), a[i + s])
            a = nxt
        base = lax.rem(q, 2) * 512 + (q // 2) * 16
        for b in range(16):
            ff[pl.ds(base + b, 16, 32), :] = a[b]

    loop(4, swap)
    mine = pl.ds(pl.multiple_of(gy * 32, 32), 32)

    def own_block(t):
        wk[t, mine, :] = ff[pl.ds(pl.multiple_of(t * 32, 32), 32), :].astype(BF16)

    loop(28, own_block)

    def block(g):
        return wk.at[:, pl.ds(pl.multiple_of(g * 32, 32), 32), :]

    def gather_y(k):
        return remote(block(gy), block(gy), bs.at[k], br.at[k], gx, lax.rem(gy + 2 * k, NY))

    def gather_y_in(k):
        return remote(
            block(lax.rem(gy + NY - 2 * k, NY)), block(lax.rem(gy + NY - 2 * k, NY)), bs.at[k], br.at[k], gx, sib
        )

    def pass_on(k):
        src = lax.rem(gy + NY - 2 * k, NY)
        return remote(block(src), block(src), fs.at[k], fr.at[k], gx, sib)

    def pass_in(k):
        src = lax.rem(sib + NY - 2 * k, NY)
        return remote(block(src), block(src), fs.at[k], fr.at[k], gx, sib)

    for k in (2, 1, 3):
        gather_y(k).start()
    pass_on(0).start()

    plane_up.wait_recv()
    load_plane(rh.at[0], 0, has_xdn)
    load_plane(v.at[0], 1, None)
    turn(0)
    first = rows_out(1, 0, 1)
    for c in first:
        c.start()
    plane_dn.wait_recv()
    load_plane(v.at[5], 0, None)
    load_plane(rh.at[1], 1, has_xup)
    turn(3)
    last = rows_out(2, 3, 1)
    for c in last:
        c.start()
    section3(1, 1)
    for c in first:
        c.wait_recv()
    for d in range(2):
        place_row(d, 0)
    section3(0, 0)
    section3(0, 1)
    pooled_dn = remote(x4.at[1, 1, pl.ds(1, 8)], ph.at[1], phs.at[1], phr.at[1], xdn, gy)
    pooled_dn.start()
    for c in last:
        c.wait_recv()
    for d in range(2):
        place_row(d, 3)
    section3(2, 0)
    section3(2, 1)
    pooled_up = remote(x4.at[1, 3, pl.ds(1, 8)], ph.at[0], phs.at[0], phr.at[0], xup, gy)
    pooled_up.start()

    def pooled_rows(n, plane, count):
        up = remote(x4.at[1, pl.ds(plane, count), 8], pr.at[0, pl.ds(plane, count)], prs.at[n, 0], prr.at[n, 0], gx, yup)
        dn = remote(x4.at[1, pl.ds(plane, count), 1], pr.at[1, pl.ds(plane, count)], prs.at[n, 1], prr.at[n, 1], gx, ydn)
        return up, dn

    def place_pooled_row(d, plane):
        place_pooled(pr[d, plane].astype(F32) * (has_ydn if d == 0 else has_yup), plane, 9 * d)

    mid = pooled_rows(0, 1, 3)
    for c in mid:
        c.start()
    for k in (1, 3, 2):
        gather_y_in(k).wait_recv()
        pass_on(k).start()

    pooled_dn.wait_recv()
    loop(8, lambda r: place_pooled(ph[1, r].astype(F32) * has_xup, 4, r + 1))
    high = pooled_rows(2, 4, 1)
    for c in high:
        c.start()
    pooled_up.wait_recv()
    loop(8, lambda r: place_pooled(ph[0, r].astype(F32) * has_xdn, 0, r + 1))
    low = pooled_rows(1, 0, 1)
    for c in low:
        c.start()
    for c in mid:
        c.wait_recv()
    for plane in (1, 2, 3):
        for d in range(2):
            place_pooled_row(d, plane)
    for k in (0, 1, 3, 2):
        pass_in(k).wait_recv()

    def send_out(d, k):
        to = lax.rem(gy + k + 1, NY)
        return remote(
            ob.at[d, pl.ds(pl.multiple_of(to * 32, 32), 32)],
            out.at[d, :, pl.ds(pl.multiple_of(gy * 512, 512), 512)],
            os_.at[d, k], or_.at[d, k], gx, to,
        )

    def come_in(d, k):
        src = lax.rem(gy + NY - k - 1, NY)
        return remote(
            ob.at[d, pl.ds(pl.multiple_of(gy * 32, 32), 32)],
            out.at[d, :, pl.ds(pl.multiple_of(src * 512, 512), 512)],
            os_.at[d, k], or_.at[d, k], gx, src,
        )

    def keep(d):
        return pltpu.make_async_copy(
            ob.at[d, pl.ds(pl.multiple_of(gy * 32, 32), 32)],
            out.at[d, :, pl.ds(pl.multiple_of(gy * 512, 512), 512)],
            ol.at[d],
        )

    def section4(d):
        hot = jnp.where(lax.broadcasted_iota(jnp.int32, (512, 128), 1) == 0, 1.0, 0.0).astype(BF16)
        acc = None
        for t in range(0, 28, 2):
            xs = []
            for u in (t, t + 1):
                kd, kh, kw = u // 9, u // 3 % 3, u % 3
                xs.append(hot if u == 27 else x4[kw, d + kd, pl.ds(kh, 8)].reshape(512, 128))
            part = lax.dot_general(
                jnp.concatenate([wk[t], wk[t + 1]], 1), jnp.concatenate(xs, 1), NT, preferred_element_type=F32
            )
            acc = part if acc is None else acc + part
        ob[d] = jnp.where(acc > 0, acc, 0.3 * acc).astype(BF16)
        loop(NY - 1, lambda k: send_out(d, k).start())
        keep(d).start()

    section4(1)
    for c in low:
        c.wait_recv()
    for d in range(2):
        place_pooled_row(d, 0)
    section4(0)
    for c in high:
        c.wait_recv()
    for d in range(2):
        place_pooled_row(d, 4)
    section4(2)

    for c in (plane_up, plane_dn, *inner, *first, *last, pooled_up, pooled_dn, *mid, *low, *high):
        c.wait_send()
    loop(NX - 1, lambda k: gather_x(k).wait_send())
    for k in (1, 2, 3):
        gather_y(k).wait_send()
    for k in (0, 1, 2, 3):
        pass_on(k).wait_send()
    for d in (1, 0, 2):
        loop(NY - 1, lambda k: send_out(d, k).wait_send())
        keep(d).wait()
    for d in (1, 0, 2):
        loop(NY - 1, lambda k: come_in(d, k).wait_recv())


def on_device(volume, weight3, bias3, weight4, bias4):
    vmem = pl.BlockSpec(memory_space=pltpu.VMEM)
    anywhere = pl.BlockSpec(memory_space=pl.ANY)
    dma = pltpu.SemaphoreType.DMA
    return pl.pallas_call(
        kernel,
        out_shape=jax.ShapeDtypeStruct((3, 32, 4096), BF16),
        in_specs=[anywhere, vmem, vmem, vmem, vmem],
        out_specs=anywhere,
        scratch_shapes=[
            pltpu.VMEM((6, 64, 16, 128), BF16),
            pltpu.VMEM((2, 64, 16, 128), BF16),
            pltpu.VMEM((2048, 128), F32),
            pltpu.VMEM((4, 144, 128), F32),
            pltpu.VMEM((3, 4, 18, 128, 128), BF16),
            pltpu.VMEM((2, 4, 128, 128), BF16),
            pltpu.VMEM((4096, 128), F32),
            pltpu.VMEM((256, 2304), BF16),
            pltpu.VMEM((3, 5, 10, 64, 128), BF16),
            pltpu.VMEM((2, 8, 64, 128), BF16),
            pltpu.VMEM((2, 5, 64, 128), BF16),
            pltpu.VMEM((4, 128, 128), F32),
            pltpu.VMEM((1024, 128), F32),
            pltpu.VMEM((16, 64, 128), BF16),
            pltpu.VMEM((1024, 128), F32),
            pltpu.VMEM((28, 256, 128), BF16),
            pltpu.VMEM((3, 256, 512), BF16),
            dma(()),
            dma((2,)), dma((2,)),
            dma((3, 2)), dma((3, 2)),
            dma((NX - 1,)), dma((NX - 1,)),
            dma((4,)), dma((4,)),
            dma((4,)), dma((4,)),
            dma((2,)), dma((2,)),
            dma((3, 2)), dma((3, 2)),
            dma((3, NY - 1)), dma((3, NY - 1)),
            dma((3,)),
        ],
        compiler_params=pltpu.CompilerParams(
            collective_id=0, has_side_effects=True, vmem_limit_bytes=58 * 2**20
        ),
        name="encoder",
    )(volume, weight3, bias3.reshape(1, 128), weight4, bias4.reshape(1, 32))


def solution(mesh):
    return jax.shard_map(
        on_device,
        mesh=mesh,
        in_specs=(P("gx", None, "gy", None), P(), P(), P("gy", None, "gx"), P("gy")),
        out_specs=P("gx", "gy", None),
        check_vma=False,
    )
```

```python
import jax
import jax.numpy as jnp
from jax import lax
from jax.experimental import pallas as pl
from jax.experimental.pallas import tpu as pltpu
from jax.sharding import PartitionSpec as P

MESH = pl.DeviceIdType.MESH
F32 = jnp.float32
BF16 = jnp.bfloat16
NT = (((1,), (1,)), ((), ()))
NN = (((1,), (0,)), ((), ()))
NX = 16
NY = 8


def remote(src, dst, send, recv, gx, gy):
    return pltpu.make_async_remote_copy(
        src_ref=src, dst_ref=dst, send_sem=send, recv_sem=recv, device_id=(gx, gy), device_id_type=MESH
    )


def loop(count, step):
    lax.fori_loop(0, count, lambda i, c: (step(i), c)[1], 0)


def kernel(
    vol, w3, b3, w4, b4, out,
    v, vs, tt, xt, q, rq, rr, rc, w3n, x4, ph, pr, pt, ws, ga, wk, ob,
    lsem, hs, hr, rs, rrs, as_, ar, bs, br, fs, fr, phs, phr, prs, prr, os_, or_, ol,
):
    gx = lax.axis_index("gx")
    gy = lax.axis_index("gy")
    xup, xdn = lax.rem(gx + 1, NX), lax.rem(gx + NX - 1, NX)
    yup, ydn = lax.rem(gy + 1, NY), lax.rem(gy + NY - 1, NY)
    sib = gy + 1 - 2 * lax.rem(gy, 2)
    has_xdn = (gx > 0).astype(F32)
    has_xup = (gx < NX - 1).astype(F32)
    has_ydn = (gy > 0).astype(F32)
    has_yup = (gy < NY - 1).astype(F32)

    barrier = pltpu.get_barrier_semaphore()

    def greet_x(k):
        pl.semaphore_signal(barrier, inc=1, device_id=(lax.rem(gx + k + 1, NX), gy), device_id_type=MESH)

    def greet_y(k):
        pl.semaphore_signal(barrier, inc=1, device_id=(gx, lax.rem(gy + k + 1, NY)), device_id_type=MESH)

    loop(NX - 1, greet_x)
    loop(NY - 1, greet_y)
    for dx in (xup, xdn):
        for dy in (yup, ydn):
            pl.semaphore_signal(barrier, inc=1, device_id=(dx, dy), device_id_type=MESH)
    local_vol = pltpu.make_async_copy(vol, v, lsem)
    local_vol.start()

    ws[...] = jnp.zeros_like(ws)
    ws[0:216, 0:32] = w4[...].astype(F32).reshape(216, 32)
    ws[216:217, 0:32] = b4[...].astype(F32)
    for t in range(2):
        ga[gx, t] = ws[t * 128 : (t + 1) * 128, :].T[0:32].astype(BF16)

    blank = jnp.zeros((64, 128), BF16)
    for n in range(9):
        for s in range(2):
            for p in range(4):
                tap = w3[9 * (p - s) + n] if 0 <= p - s < 3 else blank
                w3n[n * 256 + p * 64 : n * 256 + p * 64 + 64, s * 128 : (s + 1) * 128] = tap

    tt[...] = jnp.zeros_like(tt)

    def load_plane(src, half):
        def step(i):
            vs[pl.ds(half * 1024 + i * 128, 128), :] = src[pl.ds(i * 8, 8)].astype(F32).reshape(128, 128)

        loop(8, step)

    def place(x, u, j, h):
        tt[u, 8:136] = x
        for kw in range(3):
            xt[kw, j, h] = tt[u, 7 + kw : 135 + kw].astype(BF16)

    def turn(j):
        def step(i):
            for u in range(4):
                h = i * 4 + u
                place(vs[pl.ds(h, 128, 16), :].T, u, j, h + 1)

        loop(4, step)

    def turn_outer(n):
        def step(i):
            for u in range(2):
                r = i * 2 + u
                pair = jnp.concatenate(
                    [vs[pl.ds(n * 1024 + 2 * r, 64, 16), :], vs[pl.ds(n * 1024 + 2 * r + 1, 64, 16), :]], 0
                )
                q[n, r] = pair.T.astype(BF16)

        loop(4, step)

    left = lax.broadcasted_iota(jnp.int32, (128, 128), 1) < 64

    def merge(lo, hi, odd):
        if odd:
            return jnp.where(left, pltpu.roll(lo, 64, 1), hi)
        return jnp.where(left, lo, pltpu.roll(hi, 64, 1))

    local_vol.wait()
    for j in (1, 2):
        load_plane(v.at[2 * j - 1], 0)
        load_plane(v.at[2 * j], 1)
        turn(j)
    for n in range(2):
        load_plane(v.at[5 * n], n)
    for n in range(2):
        turn_outer(n)

    def section3(j, tops):
        def rows(kw, p, kh):
            if len(tops) == 1:
                return xt[kw, p, pl.ds(2 * tops[0] + kh, 8)].reshape(1024, 128)
            return jnp.concatenate([xt[kw, p, pl.ds(2 * t + kh, 4)].reshape(512, 128) for t in tops], 0)

        acc = None
        for kh in range(3):
            parts = []
            for kw in range(3):
                parts.append(rows(kw, j, kh))
                parts.append(rows(kw, j + 1, kh))
            d = lax.dot_general(
                jnp.concatenate(parts, 1), w3n[kh * 768 : (kh + 1) * 768, :], NN, preferred_element_type=F32
            )
            acc = d if acc is None else acc + d
        m = jnp.maximum(acc[:, :128], acc[:, 128:]).reshape(4, 2, 128, 128)
        bias = b3[...].astype(F32)
        for i in range(4):
            pt[i] = jnp.maximum(m[i, 0], m[i, 1])
            p = jnp.maximum(pt[i, pl.ds(0, 64, 2), :], pt[i, pl.ds(1, 64, 2), :])
            place_pooled(jnp.maximum(p + bias, 0.0), j + 1, tops[0] + i + 1 if len(tops) == 1 else tops[i // 2] + i % 2 + 1)

    def place_pooled(p, plane, r):
        z = jnp.zeros((1, 128), F32)
        x4[0, plane, r] = jnp.concatenate([z, p[:-1]], 0).astype(BF16)
        x4[1, plane, r] = p.astype(BF16)
        x4[2, plane, r] = jnp.concatenate([p[1:], z], 0).astype(BF16)

    pl.semaphore_wait(barrier, NX - 1 + NY - 1 + 4)

    def planes_out(part):
        r = pl.ds(0, 5) if part == 0 else pl.ds(5, 3)
        up = remote(q.at[1, r], rq.at[0, r], hs.at[0, part], hr.at[0, part], xup, gy)
        dn = remote(q.at[0, r], rq.at[1, r], hs.at[1, part], hr.at[1, part], xdn, gy)
        return up, dn

    def rows_out(d):
        y = (yup, ydn)[d]
        r = (7, 0)[d]
        return (
            remote(xt.at[1, pl.ds(1, 2), (16, 1)[d]], rr.at[d], rs.at[0, d], rrs.at[0, d], gx, y),
            remote(q.at[:, r], rc.at[d, pl.ds(1, 2)], rs.at[1, d], rrs.at[1, d], gx, y),
            remote(q.at[1, r], rc.at[d, 0], rs.at[2, d], rrs.at[2, d], xup, y),
            remote(q.at[0, r], rc.at[d, 3], rs.at[3, d], rrs.at[3, d], xdn, y),
        )

    def gather_x(k):
        return remote(ga.at[gx], ga.at[gx], as_.at[k], ar.at[k], lax.rem(gx + k + 1, NX), gy)

    def gather_x_in(k):
        src = lax.rem(gx + NX - k - 1, NX)
        return remote(ga.at[src], ga.at[src], as_.at[k], ar.at[k], gx, gy)

    outer = [planes_out(0), planes_out(1)]
    edge = [rows_out(0), rows_out(1)]
    for d in range(2):
        edge[d][0].start()
    for c in outer[0]:
        c.start()
    loop(NX - 1, lambda k: gather_x(k).start())
    for d in range(2):
        for c in edge[d][1:]:
            c.start()
    for c in outer[1]:
        c.start()

    section3(1, (2,))
    for d in range(2):
        edge[d][0].wait_recv()
        for j in (1, 2):
            place(rr[d, j - 1].astype(F32) * (has_ydn, has_yup)[d], 2 * d + j - 1, j, 17 * d)
    section3(1, (0, 6))

    loop(NX - 1, lambda k: gather_x_in(k).wait_recv())
    lane_group = lax.broadcasted_iota(jnp.int32, (16, 128), 1) // 8

    def swap(q):
        t = q // 2
        half = pl.multiple_of(lax.rem(q, 2) * 16, 16)
        a = [ga[i, t, pl.ds(half, 16)].astype(F32) for i in range(16)]
        for s in (1, 2, 4, 8):
            low = (lane_group // s) % 2 == 0
            nxt = list(a)
            for i in range(16):
                if i & s == 0:
                    nxt[i] = jnp.where(low, a[i], pltpu.roll(a[i + s], 8 * s, 1))
                    nxt[i + s] = jnp.where(low, pltpu.roll(a[i], 128 - 8 * s, 1), a[i + s])
            a = nxt
        for i in range(16):
            wk[t * 16 + i, pl.ds(pl.multiple_of(gy * 32 + half, 16), 16), :] = a[i].astype(BF16)

    loop(4, swap)

    def block(g):
        return wk.at[pl.ds(0, 28), pl.ds(pl.multiple_of(g * 32, 32), 32), :]

    def gather_y(k):
        return remote(block(gy), block(gy), bs.at[k], br.at[k], gx, lax.rem(gy + 2 * k, NY))

    def gather_y_in(k):
        return remote(
            block(lax.rem(gy + NY - 2 * k, NY)), block(lax.rem(gy + NY - 2 * k, NY)), bs.at[k], br.at[k], gx, sib
        )

    def pass_on(k):
        src = lax.rem(gy + NY - 2 * k, NY)
        return remote(block(src), block(src), fs.at[k], fr.at[k], gx, sib)

    def pass_in(k):
        src = lax.rem(sib + NY - 2 * k, NY)
        return remote(block(src), block(src), fs.at[k], fr.at[k], gx, sib)

    for k in (2, 1, 3):
        gather_y(k).start()
    pass_on(0).start()

    def merge_rows(j, lo, hi):
        def step(r):
            for odd in range(2):
                x = merge(lo(r), hi(r), odd)
                place(x, odd + 2 * (j // 3), j, 2 * r + odd + 1)

        return step

    def span(first, count, step):
        lax.fori_loop(first, first + count, lambda i, c: (step(i), c)[1], 0)

    def outer_rows(first, count):
        span(first, count, merge_rows(0, lambda r: rq[0, r].astype(F32) * has_xdn, lambda r: q[0, r].astype(F32)))
        span(first, count, merge_rows(3, lambda r: q[1, r].astype(F32), lambda r: rq[1, r].astype(F32) * has_xup))

    def edge_rows(d):
        for c in edge[d][1:]:
            c.wait_recv()
        have = (has_ydn, has_yup)[d]
        b = [rc[d, i].astype(F32) for i in range(4)]
        place(merge(b[0] * (have * has_xdn), b[1] * have, d == 0), 0, 0, 17 * d)
        place(merge(b[2] * have, b[3] * (have * has_xup), d == 0), 1, 3, 17 * d)

    for c in outer[0]:
        c.wait_recv()
    outer_rows(0, 5)
    edge_rows(0)
    def pooled_plane(up, half):
        r = pl.ds(4 * half, 4)
        return remote(
            x4.at[1, 3 if up else 1, pl.ds(1 + 4 * half, 4)], ph.at[1 - up, r],
            phs.at[up, half], phr.at[up, half], xup if up else xdn, gy,
        )

    def pooled_rows(d):
        y = (yup, ydn)[d]
        r = (8, 1)[d]
        return (
            remote(x4.at[1, pl.ds(1, 3), r], pr.at[d, pl.ds(1, 3)], prs.at[0, d], prr.at[0, d], gx, y),
            remote(x4.at[1, 3, r], pr.at[d, 0], prs.at[1, d], prr.at[1, d], xup, y),
            remote(x4.at[1, 1, r], pr.at[d, 4], prs.at[2, d], prr.at[2, d], xdn, y),
        )

    def place_pooled_row(d, plane):
        have = has_yup if d else has_ydn
        if plane in (0, 4):
            have = have * (has_xup if plane else has_xdn)
        place_pooled(pr[d, plane].astype(F32) * have, plane, 9 * d)

    def place_pooled_plane(up, half):
        pooled_plane(up, half).wait_recv()
        have, plane = (has_xdn, 0) if up else (has_xup, 4)
        for i in range(4):
            r = half * 4 + i
            place_pooled(ph[1 - up, r].astype(F32) * have, plane, r + 1)

    rim = [pooled_rows(0), pooled_rows(1)]
    section3(0, (0,))
    pooled_plane(0, 0).start()
    section3(2, (0,))
    pooled_plane(1, 0).start()
    for c in rim[1]:
        c.start()
    for c in outer[1]:
        c.wait_recv()
    outer_rows(5, 3)
    edge_rows(1)
    section3(0, (4,))
    pooled_plane(0, 1).start()
    section3(2, (4,))
    rim[0][0].start()
    pooled_plane(1, 1).start()
    for c in rim[0][1:]:
        c.start()
    for k in (1, 3, 2):
        gather_y_in(k).wait_recv()
        pass_on(k).start()
    rim[1][0].wait_recv()
    for plane in (1, 2, 3):
        place_pooled_row(1, plane)
    for k in (0, 1, 3, 2):
        pass_in(k).wait_recv()

    def span_of(g, half):
        return pl.ds(pl.multiple_of(g * 512 + 256 * half, 256), 256)

    def result(d, half, g):
        return ob.at[d, half, pl.ds(pl.multiple_of(g * 32, 32), 32)]

    def send_out(d, half, k):
        to = lax.rem(gy + k + 1, NY)
        return remote(
            result(d, half, to), out.at[d, :, span_of(gy, half)], os_.at[d, half, k], or_.at[d, half, k], gx, to
        )

    def come_in(d, half, k):
        src = lax.rem(gy + NY - k - 1, NY)
        return remote(
            result(d, half, gy), out.at[d, :, span_of(src, half)], os_.at[d, half, k], or_.at[d, half, k], gx, src
        )

    def keep(d, half):
        return pltpu.make_async_copy(result(d, half, gy), out.at[d, :, span_of(gy, half)], ol.at[d, half])

    hot = jnp.where(lax.broadcasted_iota(jnp.int32, (256, 128), 1) == 0, 1.0, 0.0).astype(BF16)

    def section4(d, half):
        acc = None
        for t in range(0, 28, 2):
            xs = []
            for u in (t, t + 1):
                kd, kh, kw = u // 9, u // 3 % 3, u % 3
                xs.append(hot if u == 27 else x4[kw, d + kd, pl.ds(4 * half + kh, 4)].reshape(256, 128))
            part = lax.dot_general(
                jnp.concatenate([wk[t], wk[t + 1]], 1), jnp.concatenate(xs, 1), NT, preferred_element_type=F32
            )
            acc = part if acc is None else acc + part
        ob[d, half] = jnp.where(acc > 0, acc, 0.3 * acc).astype(BF16)
        loop(NY - 1, lambda k: send_out(d, half, k).start())
        keep(d, half).start()

    section4(1, 1)
    rim[0][0].wait_recv()
    for plane in (1, 2, 3):
        place_pooled_row(0, plane)
    section4(1, 0)
    place_pooled_plane(0, 0)
    place_pooled_plane(0, 1)
    rim[1][2].wait_recv()
    place_pooled_row(1, 4)
    section4(2, 1)
    rim[0][2].wait_recv()
    place_pooled_row(0, 4)
    section4(2, 0)
    place_pooled_plane(1, 0)
    place_pooled_plane(1, 1)
    rim[1][1].wait_recv()
    place_pooled_row(1, 0)
    section4(0, 1)
    rim[0][1].wait_recv()
    place_pooled_row(0, 0)
    section4(0, 0)

    for c in (*outer[0], *outer[1], *edge[0], *edge[1], *rim[0], *rim[1]):
        c.wait_send()
    for up in range(2):
        for half in range(2):
            pooled_plane(up, half).wait_send()
    loop(NX - 1, lambda k: gather_x(k).wait_send())
    for k in (1, 2, 3):
        gather_y(k).wait_send()
    for k in (0, 1, 2, 3):
        pass_on(k).wait_send()
    parts = [(d, half) for d in (1, 2, 0) for half in (1, 0)]
    for d, half in parts:
        loop(NY - 1, lambda k: send_out(d, half, k).wait_send())
        keep(d, half).wait()
    for d, half in parts:
        loop(NY - 1, lambda k: come_in(d, half, k).wait_recv())


def on_device(volume, weight3, bias3, weight4, bias4):
    vmem = pl.BlockSpec(memory_space=pltpu.VMEM)
    anywhere = pl.BlockSpec(memory_space=pl.ANY)
    dma = pltpu.SemaphoreType.DMA
    return pl.pallas_call(
        kernel,
        out_shape=jax.ShapeDtypeStruct((3, 32, 4096), BF16),
        in_specs=[anywhere, vmem, vmem, vmem, vmem],
        out_specs=anywhere,
        scratch_shapes=[
            pltpu.VMEM((6, 64, 16, 128), BF16),
            pltpu.VMEM((2048, 128), F32),
            pltpu.VMEM((4, 144, 128), F32),
            pltpu.VMEM((3, 4, 18, 128, 128), BF16),
            pltpu.VMEM((2, 8, 128, 128), BF16),
            pltpu.VMEM((2, 8, 128, 128), BF16),
            pltpu.VMEM((2, 2, 128, 128), BF16),
            pltpu.VMEM((2, 4, 128, 128), BF16),
            pltpu.VMEM((2304, 256), BF16),
            pltpu.VMEM((3, 5, 10, 64, 128), BF16),
            pltpu.VMEM((2, 8, 64, 128), BF16),
            pltpu.VMEM((2, 5, 64, 128), BF16),
            pltpu.VMEM((4, 128, 128), F32),
            pltpu.VMEM((256, 128), F32),
            pltpu.VMEM((16, 2, 32, 128), BF16),
            pltpu.VMEM((32, 256, 128), BF16),
            pltpu.VMEM((3, 2, 256, 256), BF16),
            dma(()),
            dma((2, 2)), dma((2, 2)),
            dma((4, 2)), dma((4, 2)),
            dma((NX - 1,)), dma((NX - 1,)),
            dma((4,)), dma((4,)),
            dma((4,)), dma((4,)),
            dma((2, 2)), dma((2, 2)),
            dma((3, 2)), dma((3, 2)),
            dma((3, 2, NY - 1)), dma((3, 2, NY - 1)),
            dma((3, 2)),
        ],
        compiler_params=pltpu.CompilerParams(
            collective_id=0, has_side_effects=True, vmem_limit_bytes=58 * 2**20
        ),
        name="encoder",
    )(volume, weight3.transpose(1, 2, 0), bias3.reshape(1, 128), weight4.transpose(1, 2, 0), bias4.reshape(1, 32))


def solution(mesh):
    return jax.shard_map(
        on_device,
        mesh=mesh,
        in_specs=(P("gx", None, "gy", None), P(), P(), P("gy", None, "gx"), P("gy")),
        out_specs=P("gx", "gy", None),
        check_vma=False,
    )
```

```python
import jax
import jax.numpy as jnp
from jax import lax
from jax.experimental import pallas as pl
from jax.experimental.pallas import tpu as pltpu
from jax.sharding import PartitionSpec as P

MESH = pl.DeviceIdType.MESH
F32 = jnp.float32
BF16 = jnp.bfloat16
NT = (((1,), (1,)), ((), ()))
NN = (((1,), (0,)), ((), ()))
NX = 16
NY = 8


def remote(src, dst, send, recv, gx, gy):
    return pltpu.make_async_remote_copy(
        src_ref=src, dst_ref=dst, send_sem=send, recv_sem=recv, device_id=(gx, gy), device_id_type=MESH
    )


def loop(count, step):
    lax.fori_loop(0, count, lambda i, c: (step(i), c)[1], 0)


def kernel(
    vol, w3, b3, w4, b4, out,
    v, vs, tt, xt, q, rq, rr, rc, w3n, x4, ph, pr, pt, ws, ga, wk, ob,
    lsem, hs, hr, rs, rrs, as_, ar, bs, br, fs, fr, phs, phr, prs, prr, os_, or_, ol,
):
    gx = lax.axis_index("gx")
    gy = lax.axis_index("gy")
    xup, xdn = lax.rem(gx + 1, NX), lax.rem(gx + NX - 1, NX)
    yup, ydn = lax.rem(gy + 1, NY), lax.rem(gy + NY - 1, NY)
    sib = gy + 1 - 2 * lax.rem(gy, 2)
    has_xdn = (gx > 0).astype(F32)
    has_xup = (gx < NX - 1).astype(F32)
    has_ydn = (gy > 0).astype(F32)
    has_yup = (gy < NY - 1).astype(F32)

    barrier = pltpu.get_barrier_semaphore()

    def greet_x(k):
        pl.semaphore_signal(barrier, inc=1, device_id=(lax.rem(gx + k + 1, NX), gy), device_id_type=MESH)

    def greet_y(k):
        pl.semaphore_signal(barrier, inc=1, device_id=(gx, lax.rem(gy + k + 1, NY)), device_id_type=MESH)

    loop(NX - 1, greet_x)
    loop(NY - 1, greet_y)
    for dx in (xup, xdn):
        for dy in (yup, ydn):
            pl.semaphore_signal(barrier, inc=1, device_id=(dx, dy), device_id_type=MESH)
    local_vol = pltpu.make_async_copy(vol, v, lsem)
    local_vol.start()

    ws[...] = jnp.zeros_like(ws)
    ws[0:216, 0:32] = w4[...].astype(F32).reshape(216, 32)
    ws[216:217, 0:32] = b4[...].astype(F32)
    for t in range(2):
        ga[gx, t] = ws[t * 128 : (t + 1) * 128, :].T[0:32].astype(BF16)

    tt[...] = jnp.zeros_like(tt)

    def load_plane(src, half):
        def step(i):
            vs[pl.ds(half * 1024 + i * 128, 128), :] = src[pl.ds(i * 8, 8)].astype(F32).reshape(128, 128)

        loop(8, step)

    def place(x, u, j, h):
        tt[u, 8:136] = x
        for kw in range(3):
            xt[kw, j, h] = tt[u, 7 + kw : 135 + kw].astype(BF16)

    def turn(j):
        def step(i):
            for u in range(4):
                h = i * 4 + u
                place(vs[pl.ds(h, 128, 16), :].T, u, j, h + 1)

        loop(4, step)

    def turn_outer(n):
        def step(i):
            for u in range(2):
                r = i * 2 + u
                pair = jnp.concatenate(
                    [vs[pl.ds(n * 1024 + 2 * r, 64, 16), :], vs[pl.ds(n * 1024 + 2 * r + 1, 64, 16), :]], 0
                )
                q[n, r] = pair.T.astype(BF16)

        loop(4, step)

    left = lax.broadcasted_iota(jnp.int32, (128, 128), 1) < 64

    def merge(lo, hi, odd):
        if odd:
            return jnp.where(left, pltpu.roll(lo, 64, 1), hi)
        return jnp.where(left, lo, pltpu.roll(hi, 64, 1))

    local_vol.wait()
    for n in range(2):
        load_plane(v.at[5 * n], n)
    for n in range(2):
        turn_outer(n)

    def section3(j, tops):
        def rows(kw, p, kh):
            if len(tops) == 1:
                return xt[kw, p, pl.ds(2 * tops[0] + kh, 8)].reshape(1024, 128)
            return jnp.concatenate([xt[kw, p, pl.ds(2 * t + kh, 4)].reshape(512, 128) for t in tops], 0)

        acc = None
        for kh in range(3):
            parts = []
            for kw in range(3):
                parts.append(rows(kw, j, kh))
                parts.append(rows(kw, j + 1, kh))
            d = lax.dot_general(
                jnp.concatenate(parts, 1), w3n[kh * 768 : (kh + 1) * 768, :], NN, preferred_element_type=F32
            )
            acc = d if acc is None else acc + d
        m = jnp.maximum(acc[:, :128], acc[:, 128:]).reshape(4, 2, 128, 128)
        bias = b3[...].astype(F32)
        for i in range(4):
            pt[i] = jnp.maximum(m[i, 0], m[i, 1])
            p = jnp.maximum(pt[i, pl.ds(0, 64, 2), :], pt[i, pl.ds(1, 64, 2), :])
            place_pooled(jnp.maximum(p + bias, 0.0), j + 1, tops[0] + i + 1 if len(tops) == 1 else tops[i // 2] + i % 2 + 1)

    def place_pooled(p, plane, r):
        z = jnp.zeros((1, 128), F32)
        x4[0, plane, r] = jnp.concatenate([z, p[:-1]], 0).astype(BF16)
        x4[1, plane, r] = p.astype(BF16)
        x4[2, plane, r] = jnp.concatenate([p[1:], z], 0).astype(BF16)

    pl.semaphore_wait(barrier, NX - 1 + NY - 1 + 4)

    def planes_out(part):
        r = pl.ds(0, 5) if part == 0 else pl.ds(5, 3)
        up = remote(q.at[1, r], rq.at[0, r], hs.at[0, part], hr.at[0, part], xup, gy)
        dn = remote(q.at[0, r], rq.at[1, r], hs.at[1, part], hr.at[1, part], xdn, gy)
        return up, dn

    def rows_out(d):
        y = (yup, ydn)[d]
        r = (7, 0)[d]
        return (
            remote(xt.at[1, pl.ds(1, 2), (16, 1)[d]], rr.at[d], rs.at[0, d], rrs.at[0, d], gx, y),
            remote(q.at[:, r], rc.at[d, pl.ds(1, 2)], rs.at[1, d], rrs.at[1, d], gx, y),
            remote(q.at[1, r], rc.at[d, 0], rs.at[2, d], rrs.at[2, d], xup, y),
            remote(q.at[0, r], rc.at[d, 3], rs.at[3, d], rrs.at[3, d], xdn, y),
        )

    def gather_x(k):
        return remote(ga.at[gx], ga.at[gx], as_.at[k], ar.at[k], lax.rem(gx + k + 1, NX), gy)

    def gather_x_in(k):
        src = lax.rem(gx + NX - k - 1, NX)
        return remote(ga.at[src], ga.at[src], as_.at[k], ar.at[k], gx, gy)

    outer = [planes_out(0), planes_out(1)]
    edge = [rows_out(0), rows_out(1)]
    loop(NX - 1, lambda k: gather_x(k).start())
    for c in outer[0]:
        c.start()
    for d in range(2):
        for c in edge[d][1:]:
            c.start()
    for c in outer[1]:
        c.start()

    for j in (1, 2):
        load_plane(v.at[2 * j - 1], 0)
        load_plane(v.at[2 * j], 1)
        turn(j)
    for d in range(2):
        edge[d][0].start()

    blank = jnp.zeros((64, 128), BF16)
    for n in range(9):
        for s in range(2):
            for p in range(4):
                tap = w3[9 * (p - s) + n] if 0 <= p - s < 3 else blank
                w3n[n * 256 + p * 64 : n * 256 + p * 64 + 64, s * 128 : (s + 1) * 128] = tap

    section3(1, (2,))
    for d in range(2):
        edge[d][0].wait_recv()
        for j in (1, 2):
            place(rr[d, j - 1].astype(F32) * (has_ydn, has_yup)[d], 2 * d + j - 1, j, 17 * d)
    section3(1, (0, 6))

    loop(NX - 1, lambda k: gather_x_in(k).wait_recv())
    lane_group = lax.broadcasted_iota(jnp.int32, (16, 128), 1) // 8

    def swap(q):
        t = q // 2
        half = pl.multiple_of(lax.rem(q, 2) * 16, 16)
        a = [ga[i, t, pl.ds(half, 16)].astype(F32) for i in range(16)]
        for s in (1, 2, 4, 8):
            low = (lane_group // s) % 2 == 0
            nxt = list(a)
            for i in range(16):
                if i & s == 0:
                    nxt[i] = jnp.where(low, a[i], pltpu.roll(a[i + s], 8 * s, 1))
                    nxt[i + s] = jnp.where(low, pltpu.roll(a[i], 128 - 8 * s, 1), a[i + s])
            a = nxt
        for i in range(16):
            wk[t * 16 + i, pl.ds(pl.multiple_of(gy * 32 + half, 16), 16), :] = a[i].astype(BF16)

    loop(4, swap)

    def block(g):
        return wk.at[pl.ds(0, 28), pl.ds(pl.multiple_of(g * 32, 32), 32), :]

    def gather_y(k):
        return remote(block(gy), block(gy), bs.at[k], br.at[k], gx, lax.rem(gy + 2 * k, NY))

    def gather_y_in(k):
        return remote(
            block(lax.rem(gy + NY - 2 * k, NY)), block(lax.rem(gy + NY - 2 * k, NY)), bs.at[k], br.at[k], gx, sib
        )

    def pass_on(k):
        src = lax.rem(gy + NY - 2 * k, NY)
        return remote(block(src), block(src), fs.at[k], fr.at[k], gx, sib)

    def pass_in(k):
        src = lax.rem(sib + NY - 2 * k, NY)
        return remote(block(src), block(src), fs.at[k], fr.at[k], gx, sib)

    for k in (2, 1, 3):
        gather_y(k).start()
    pass_on(0).start()

    def merge_rows(j, lo, hi):
        def step(r):
            for odd in range(2):
                x = merge(lo(r), hi(r), odd)
                place(x, odd + 2 * (j // 3), j, 2 * r + odd + 1)

        return step

    def span(first, count, step):
        lax.fori_loop(first, first + count, lambda i, c: (step(i), c)[1], 0)

    def outer_rows(first, count):
        span(first, count, merge_rows(0, lambda r: rq[0, r].astype(F32) * has_xdn, lambda r: q[0, r].astype(F32)))
        span(first, count, merge_rows(3, lambda r: q[1, r].astype(F32), lambda r: rq[1, r].astype(F32) * has_xup))

    def edge_rows(d):
        for c in edge[d][1:]:
            c.wait_recv()
        have = (has_ydn, has_yup)[d]
        b = [rc[d, i].astype(F32) for i in range(4)]
        place(merge(b[0] * (have * has_xdn), b[1] * have, d == 0), 0, 0, 17 * d)
        place(merge(b[2] * have, b[3] * (have * has_xup), d == 0), 1, 3, 17 * d)

    for c in outer[0]:
        c.wait_recv()
    outer_rows(0, 5)
    edge_rows(0)
    def pooled_plane(up, half):
        r = pl.ds(4 * half, 4)
        return remote(
            x4.at[1, 3 if up else 1, pl.ds(1 + 4 * half, 4)], ph.at[1 - up, r],
            phs.at[up, half], phr.at[up, half], xup if up else xdn, gy,
        )

    def pooled_rows(d):
        y = (yup, ydn)[d]
        r = (8, 1)[d]
        return (
            remote(x4.at[1, pl.ds(1, 3), r], pr.at[d, pl.ds(1, 3)], prs.at[0, d], prr.at[0, d], gx, y),
            remote(x4.at[1, 3, r], pr.at[d, 0], prs.at[1, d], prr.at[1, d], xup, y),
            remote(x4.at[1, 1, r], pr.at[d, 4], prs.at[2, d], prr.at[2, d], xdn, y),
        )

    def place_pooled_row(d, plane):
        have = has_yup if d else has_ydn
        if plane in (0, 4):
            have = have * (has_xup if plane else has_xdn)
        place_pooled(pr[d, plane].astype(F32) * have, plane, 9 * d)

    def place_pooled_plane(up, half):
        pooled_plane(up, half).wait_recv()
        have, plane = (has_xdn, 0) if up else (has_xup, 4)
        for i in range(4):
            r = half * 4 + i
            place_pooled(ph[1 - up, r].astype(F32) * have, plane, r + 1)

    rim = [pooled_rows(0), pooled_rows(1)]
    section3(0, (0,))
    pooled_plane(0, 0).start()
    section3(2, (0,))
    pooled_plane(1, 0).start()
    for c in rim[1]:
        c.start()
    for c in outer[1]:
        c.wait_recv()
    outer_rows(5, 3)
    edge_rows(1)
    section3(0, (4,))
    pooled_plane(0, 1).start()
    section3(2, (4,))
    rim[0][0].start()
    pooled_plane(1, 1).start()
    for c in rim[0][1:]:
        c.start()
    for k in (1, 3, 2):
        gather_y_in(k).wait_recv()
        pass_on(k).start()
    rim[1][0].wait_recv()
    for plane in (1, 2, 3):
        place_pooled_row(1, plane)
    for k in (0, 1, 3, 2):
        pass_in(k).wait_recv()

    def span_of(g, half):
        return pl.ds(pl.multiple_of(g * 512 + 256 * half, 256), 256)

    def result(d, half, g):
        return ob.at[d, half, pl.ds(pl.multiple_of(g * 32, 32), 32)]

    def send_out(d, half, k):
        to = lax.rem(gy + k + 1, NY)
        return remote(
            result(d, half, to), out.at[d, :, span_of(gy, half)], os_.at[d, half, k], or_.at[d, half, k], gx, to
        )

    def come_in(d, half, k):
        src = lax.rem(gy + NY - k - 1, NY)
        return remote(
            result(d, half, gy), out.at[d, :, span_of(src, half)], os_.at[d, half, k], or_.at[d, half, k], gx, src
        )

    def keep(d, half):
        return pltpu.make_async_copy(result(d, half, gy), out.at[d, :, span_of(gy, half)], ol.at[d, half])

    hot = jnp.where(lax.broadcasted_iota(jnp.int32, (256, 128), 1) == 0, 1.0, 0.0).astype(BF16)

    def section4(d, half):
        acc = None
        for t in range(0, 28, 2):
            xs = []
            for u in (t, t + 1):
                kd, kh, kw = u // 9, u // 3 % 3, u % 3
                xs.append(hot if u == 27 else x4[kw, d + kd, pl.ds(4 * half + kh, 4)].reshape(256, 128))
            part = lax.dot_general(
                jnp.concatenate([wk[t], wk[t + 1]], 1), jnp.concatenate(xs, 1), NT, preferred_element_type=F32
            )
            acc = part if acc is None else acc + part
        ob[d, half] = jnp.where(acc > 0, acc, 0.3 * acc).astype(BF16)
        loop(NY - 1, lambda k: send_out(d, half, k).start())
        keep(d, half).start()

    section4(1, 1)
    rim[0][0].wait_recv()
    for plane in (1, 2, 3):
        place_pooled_row(0, plane)
    section4(1, 0)
    place_pooled_plane(0, 0)
    place_pooled_plane(0, 1)
    rim[1][2].wait_recv()
    place_pooled_row(1, 4)
    section4(2, 1)
    rim[0][2].wait_recv()
    place_pooled_row(0, 4)
    section4(2, 0)
    place_pooled_plane(1, 0)
    place_pooled_plane(1, 1)
    rim[1][1].wait_recv()
    place_pooled_row(1, 0)
    section4(0, 1)
    rim[0][1].wait_recv()
    place_pooled_row(0, 0)
    section4(0, 0)

    for c in (*outer[0], *outer[1], *edge[0], *edge[1], *rim[0], *rim[1]):
        c.wait_send()
    for up in range(2):
        for half in range(2):
            pooled_plane(up, half).wait_send()
    loop(NX - 1, lambda k: gather_x(k).wait_send())
    for k in (1, 2, 3):
        gather_y(k).wait_send()
    for k in (0, 1, 2, 3):
        pass_on(k).wait_send()
    parts = [(d, half) for d in (1, 2, 0) for half in (1, 0)]
    for d, half in parts:
        loop(NY - 1, lambda k: send_out(d, half, k).wait_send())
        keep(d, half).wait()
    for d, half in parts:
        loop(NY - 1, lambda k: come_in(d, half, k).wait_recv())


def on_device(volume, weight3, bias3, weight4, bias4):
    vmem = pl.BlockSpec(memory_space=pltpu.VMEM)
    anywhere = pl.BlockSpec(memory_space=pl.ANY)
    dma = pltpu.SemaphoreType.DMA
    return pl.pallas_call(
        kernel,
        out_shape=jax.ShapeDtypeStruct((3, 32, 4096), BF16),
        in_specs=[anywhere, vmem, vmem, vmem, vmem],
        out_specs=anywhere,
        scratch_shapes=[
            pltpu.VMEM((6, 64, 16, 128), BF16),
            pltpu.VMEM((2048, 128), F32),
            pltpu.VMEM((4, 144, 128), F32),
            pltpu.VMEM((3, 4, 18, 128, 128), BF16),
            pltpu.VMEM((2, 8, 128, 128), BF16),
            pltpu.VMEM((2, 8, 128, 128), BF16),
            pltpu.VMEM((2, 2, 128, 128), BF16),
            pltpu.VMEM((2, 4, 128, 128), BF16),
            pltpu.VMEM((2304, 256), BF16),
            pltpu.VMEM((3, 5, 10, 64, 128), BF16),
            pltpu.VMEM((2, 8, 64, 128), BF16),
            pltpu.VMEM((2, 5, 64, 128), BF16),
            pltpu.VMEM((4, 128, 128), F32),
            pltpu.VMEM((256, 128), F32),
            pltpu.VMEM((16, 2, 32, 128), BF16),
            pltpu.VMEM((32, 256, 128), BF16),
            pltpu.VMEM((3, 2, 256, 256), BF16),
            dma(()),
            dma((2, 2)), dma((2, 2)),
            dma((4, 2)), dma((4, 2)),
            dma((NX - 1,)), dma((NX - 1,)),
            dma((4,)), dma((4,)),
            dma((4,)), dma((4,)),
            dma((2, 2)), dma((2, 2)),
            dma((3, 2)), dma((3, 2)),
            dma((3, 2, NY - 1)), dma((3, 2, NY - 1)),
            dma((3, 2)),
        ],
        compiler_params=pltpu.CompilerParams(
            collective_id=0, has_side_effects=True, vmem_limit_bytes=58 * 2**20
        ),
        name="encoder",
    )(volume, weight3.transpose(1, 2, 0), bias3.reshape(1, 128), weight4.transpose(1, 2, 0), bias4.reshape(1, 32))


def solution(mesh):
    return jax.shard_map(
        on_device,
        mesh=mesh,
        in_specs=(P("gx", None, "gy", None), P(), P(), P("gy", None, "gx"), P("gy")),
        out_specs=P("gx", "gy", None),
        check_vma=False,
    )
```
